32 devices in a mesh: rep: 4 (over y, core), shard: 8 (over z, x).
Axes of the slice: x: 2, y: 2, z: 4, core: 2. Of those that a mesh axis runs over, the one named last changes fastest.
Arguments:
- tokens: bfloat16 [8192, 768], P(('rep', 'shard')), may hold values from -6 to 6
- seg_ids: int32 [8192], P(('rep', 'shard')), may hold values from -1 to 1, as said below
- grad_out: bfloat16 [8192, 768], P(('rep', 'shard')), may hold values from -6 to 6
- ln1_gain: bfloat16 [768], P('shard'), may hold values from 0.5 to 1.5
- ln1_bias: bfloat16 [768], P('shard'), may hold values from -1.5 to 1.5
- w_query: bfloat16 [768, 768], P('shard'), may hold values from -0.21875 to 0.21875
- w_key: bfloat16 [768, 768], P('shard'), may hold values from -0.21875 to 0.21875
- w_value: bfloat16 [768, 768], P('shard'), may hold values from -0.21875 to 0.21875
- b_query: bfloat16 [768], P('shard'), may hold values from -1.5 to 1.5
- b_value: bfloat16 [768], P('shard'), may hold values from -1.5 to 1.5
- w_out: bfloat16 [768, 768], P('shard'), may hold values from -0.875 to 0.875
- b_out: bfloat16 [768], P('shard'), may hold values from -1.5 to 1.5
- ln2_gain: bfloat16 [768], P('shard'), may hold values from 0.5 to 1.5
- ln2_bias: bfloat16 [768], P('shard'), may hold values from -1.5 to 1.5
- w_fc1: bfloat16 [768, 3072], P('shard'), may hold values from -0.21875 to 0.21875
- b_fc1: bfloat16 [3072], P('shard'), may hold values from -1.5 to 1.5
- w_fc2: bfloat16 [3072, 768], P('shard'), may hold values from -0.15625 to 0.15625
- b_fc2: bfloat16 [768], P('shard'), may hold values from -1.5 to 1.5
Outputs:
- out: bfloat16 [8192, 768], P(('rep', 'shard'))
- grad_tokens: float32 [8192, 768], P(('rep', 'shard'))
- grad_ln1_gain: float32 [768], P('shard')
- grad_ln1_bias: float32 [768], P('shard')
- grad_w_query: float32 [768, 768], P('shard')
- grad_w_key: float32 [768, 768], P('shard')
- grad_w_value: float32 [768, 768], P('shard')
- grad_b_query: float32 [768], P('shard')
- grad_b_value: float32 [768], P('shard')
- grad_w_out: float32 [768, 768], P('shard')
- grad_b_out: float32 [768], P('shard')
- grad_ln2_gain: float32 [768], P('shard')
- grad_ln2_bias: float32 [768], P('shard')
- grad_w_fc1: float32 [768, 3072], P('shard')
- grad_b_fc1: float32 [3072], P('shard')
- grad_w_fc2: float32 [3072, 768], P('shard')
- grad_b_fc2: float32 [768], P('shard')
The draws below stay inside these ranges and needn't reach their ends.
Inputs may be any that keep to these rules, and one draw needn't show every extreme that they name: `seg_ids`: within each device's 256 slots: id 0 on a first run of one or more slots, id 1 on the next run of one or more, then -1 to the end. Every device has at least 128 slots with ids 0 or 1, and some device has no -1.
All inputs are finite; a program needn't handle non-finite values.
Results may differ from the reference program's by a relative error of at most 0.012.
Values may be sent and summed in bfloat16 or wider, within the bound.
A program may use at most 128 MiB of HBM per device.

```python
import math
import jax
import jax.numpy as jnp
from jax import lax

HEADS = 12
HEAD_DIM = 64
FF = 3072
TOK_DEV = 256
D = 768
TOKENS = 8192
N_REP = 4
N_SHARD = 8


def draw_seg_ids(key, part):
    key = jax.random.fold_in(key, 7)
    key_live, key_cut, key_full = jax.random.split(key, 3)
    devices = TOKENS // TOK_DEV
    live = jax.random.randint(key_live, (devices,), TOK_DEV // 2, TOK_DEV)
    fullest = jax.random.randint(key_full, (), 0, devices)
    live = jnp.where(jnp.arange(devices) == fullest, TOK_DEV, live)
    cuts = jax.random.randint(key_cut, (devices,), 0, 1048576) % (live - 1) + 1
    order = jnp.arange(TOK_DEV)
    second = (order[None, :] >= cuts[:, None]).astype(jnp.int32)
    ids = jnp.where(order[None, :] < live[:, None], second, -1)
    return ids.reshape(TOKENS).astype(jnp.int32)


def steps_of(own_key, extent, cuts, least, high):
    def one(axis_at, parts):
        heights = jax.random.uniform(jax.random.fold_in(jax.random.fold_in(own_key, 6), axis_at), (parts,), jnp.float32, least / len(cuts), high / len(cuts))
        return jnp.repeat(jnp.exp(heights), extent[axis_at] // parts).reshape((-1,) + (1,) * (len(extent) - axis_at - 1))

    level = one(*cuts[0])
    for cut in cuts[1:]:
        level = level * one(*cut)
    return level


def scatter_about(key, shape, width, bound, shards=(), dtype=jnp.bfloat16):
    factor_of = steps_of(key, shape, shards, -0.22, 0.18) if shards else 1.0
    values = jax.random.normal(key, shape, jnp.float32) * width * factor_of
    return jnp.minimum(jnp.maximum(values, -bound), bound).astype(dtype)


def setup_inputs(seed: int = 0) -> dict:
    splits = jax.random.split(jax.random.key(seed), 19)
    return {
        "tokens": scatter_about(splits[0], (TOKENS, D), 1.0, 6.0, ((0, 32),)),
        "seg_ids": draw_seg_ids(jax.random.fold_in(splits[18], 71), 0),
        "grad_out": scatter_about(splits[2], (TOKENS, D), 1.0, 6.0, ((0, 32),)),
        "ln1_gain": jnp.clip(1.0 + 0.1 * jax.random.normal(splits[3], (D,), jnp.float32), 0.5, 1.5).astype(jnp.bfloat16),
        "ln1_bias": scatter_about(splits[4], (D,), 0.3, 1.5, ((0, 8),)),
        "w_query": scatter_about(splits[5], (D, D), D ** -0.5, 0.21875, ((0, 8),)),
        "w_key": scatter_about(splits[6], (D, D), D ** -0.5, 0.21875, ((0, 8),)),
        "w_value": scatter_about(splits[7], (D, D), D ** -0.5, 0.21875, ((0, 8),)),
        "b_query": scatter_about(splits[8], (D,), 0.3, 1.5, ((0, 8),)),
        "b_value": scatter_about(splits[9], (D,), 0.3, 1.5, ((0, 8),)),
        "w_out": scatter_about(splits[10], (D, D), (D // 16) ** -0.5, 0.875, ((0, 8),)),
        "b_out": scatter_about(splits[11], (D,), 0.3, 1.5, ((0, 8),)),
        "ln2_gain": jnp.clip(1.0 + 0.1 * jax.random.normal(splits[12], (D,), jnp.float32), 0.5, 1.5).astype(jnp.bfloat16),
        "ln2_bias": scatter_about(splits[13], (D,), 0.3, 1.5, ((0, 8),)),
        "w_fc1": scatter_about(splits[14], (D, FF), D ** -0.5, 0.21875, ((0, 8),)),
        "b_fc1": scatter_about(splits[15], (FF,), 0.3, 1.5, ((0, 8),)),
        "w_fc2": scatter_about(splits[16], (FF, D), (FF // 2) ** -0.5, 0.15625, ((0, 8),)),
        "b_fc2": scatter_about(splits[17], (D,), 0.3, 1.5, ((0, 8),)),
    }


@jax.custom_vjp
def low(v):
    return lax.optimization_barrier(v.astype(jnp.bfloat16)).astype(jnp.float32)

@jax.custom_vjp
def low_back(v):
    return v

def low_keep(v):
    return (low(v), None)

def low_pass(kept, grad):
    return (grad,)

def back_keep(v):
    return (v, None)

def back_low(kept, grad):
    return (low(grad),)
low.defvjp(low_keep, low_pass)
low_back.defvjp(back_keep, back_low)
norm_eps = 1e-05
highest = lax.Precision.HIGHEST

def layer_norm(rows, gain, shift):
    center = rows - lax.optimization_barrier(jnp.mean(rows, axis=-1, keepdims=True))
    spread = lax.optimization_barrier(jnp.mean(center * center, axis=-1, keepdims=True))
    return center * lax.rsqrt(spread + norm_eps) * gain + shift

def matmul(left, right):
    return jnp.dot(left, right, precision=highest, preferred_element_type=jnp.float32)

def attend(query, keys, values, segment):
    count = segment.shape[0]
    order = jnp.arange(count)
    allowed = (segment[:, None] == segment[None, :]) & (order[:, None] >= order[None, :])
    heads_q = query.reshape(count, HEADS, HEAD_DIM)
    heads_k = keys.reshape(count, HEADS, HEAD_DIM)
    heads_v = values.reshape(count, HEADS, HEAD_DIM)
    scores = low_back(jnp.einsum('qhd,khd->hqk', heads_q, heads_k, precision=highest)) * HEAD_DIM ** (-0.5)
    scores = jnp.where(allowed[None], scores, -1e+30)
    peak = lax.optimization_barrier(jnp.max(scores, axis=-1, keepdims=True))
    expo = jnp.exp(scores - peak)
    probs = low(expo / lax.optimization_barrier(jnp.sum(expo, axis=-1, keepdims=True)))
    mixed = jnp.einsum('hqk,khd->qhd', probs, heads_v, precision=highest)
    return mixed.reshape(count, HEADS * HEAD_DIM)

def block_forward(params, rows, segment):
    gain_one, shift_one, wq, wk, wv, bq, bv, wo, bo, gain_two, shift_two, w_one, b_one, w_two, b_two = params
    normed = low(layer_norm(rows, gain_one, shift_one))
    query = low(low_back(matmul(normed, wq) + bq))
    keys = low(low_back(matmul(normed, wk)))
    values = low(low_back(matmul(normed, wv) + bv))
    groups = rows.shape[0] // TOK_DEV
    mixed = jax.vmap(attend)(query.reshape(groups, TOK_DEV, -1), keys.reshape(groups, TOK_DEV, -1), values.reshape(groups, TOK_DEV, -1), segment.reshape(groups, TOK_DEV))
    mixed = low(low_back(mixed.reshape(rows.shape)))
    middle = rows + low_back(matmul(mixed, wo)) + bo
    normed_two = low(layer_norm(middle, gain_two, shift_two))
    hidden = low_back(matmul(normed_two, w_one) + b_one)
    active = low(jax.nn.gelu(hidden, approximate=False))
    return middle + low_back(matmul(active, w_two)) + b_two

def reference(tokens, seg_ids, grad_out, ln1_gain, ln1_bias, w_query, w_key, w_value, b_query, b_value, w_out, b_out, ln2_gain, ln2_bias, w_fc1, b_fc1, w_fc2, b_fc2):
    params = tuple((p.astype(jnp.float32) for p in (ln1_gain, ln1_bias, w_query, w_key, w_value, b_query, b_value, w_out, b_out, ln2_gain, ln2_bias, w_fc1, b_fc1, w_fc2, b_fc2)))
    rows = tokens.astype(jnp.float32)
    live = (seg_ids >= 0).astype(jnp.float32)[:, None]
    cotangent = grad_out.astype(jnp.float32) * live
    devices = N_REP * N_SHARD
    group = math.gcd(devices, 16)
    blocks = devices // group

    def forward(inputs, weights):
        blocked = inputs.reshape(blocks, group * TOK_DEV, inputs.shape[1])
        seg_blocked = seg_ids.reshape(blocks, group * TOK_DEV)
        stepper = jax.checkpoint(lambda pair: block_forward(weights, pair[0], pair[1]))
        return lax.map(stepper, (blocked, seg_blocked)).reshape(inputs.shape)
    result, pullback = jax.vjp(forward, rows, params)
    grad_rows, grads = pullback(cotangent)
    return (result.astype(jnp.bfloat16), grad_rows, grads[0], grads[1], grads[2], grads[3], grads[4], grads[5], grads[6], grads[7], grads[8], grads[9], grads[10], grads[11], grads[12], grads[13], grads[14])
```

```python
import functools

import jax
import jax.numpy as jnp
from jax import lax
from jax.experimental import pallas as pl
from jax.experimental.pallas import tpu as pltpu
from jax.sharding import PartitionSpec as P

HEADS = 12
HEAD_DIM = 64


norm_eps = 1e-05


def layer_norm(rows, gain, shift):
    center = rows - jnp.mean(rows, axis=-1, keepdims=True)
    spread = jnp.mean(center * center, axis=-1, keepdims=True)
    return center * lax.rsqrt(spread + norm_eps) * gain + shift


def gelu_exact(values):
    return jax.nn.gelu(values, approximate=False)


def product(left, right):
    return jnp.dot(left, right, preferred_element_type=jnp.float32)


def inner(left, right):
    return lax.dot_general(
        left, right, (((0,), (0,)), ((), ())), preferred_element_type=jnp.float32
    )


def against(left, right):
    return lax.dot_general(
        left, right, (((1,), (1,)), ((), ())), preferred_element_type=jnp.float32
    )


def column_sum(values):
    return jnp.sum(values.astype(jnp.float32), axis=0)


def masked_scores(heads_q, heads_k, allowed):
    scores = jnp.einsum(
        "qhd,khd->hqk", heads_q, heads_k, preferred_element_type=jnp.float32
    ) * HEAD_DIM ** (-0.5)
    return jnp.where(allowed[None], scores, -1e30)


def layer(tokens, seg_ids, grad_out, gathered):
    (
        gain_one,
        shift_one,
        wq,
        wk,
        wv,
        bq,
        bv,
        wo,
        bo,
        gain_two,
        shift_two,
        w_one,
        b_one,
        w_two,
        b_two,
    ) = gathered
    rows = tokens.astype(jnp.float32)
    count = rows.shape[0]
    width = rows.shape[1]
    order = jnp.arange(count)
    allowed = (seg_ids[:, None] == seg_ids[None, :]) & (order[:, None] >= order[None, :])
    gain_first = gain_one.astype(jnp.float32)
    shift_first = shift_one.astype(jnp.float32)
    normed = layer_norm(rows, gain_first, shift_first).astype(jnp.bfloat16)
    query = (product(normed, wq) + bq.astype(jnp.float32)).astype(jnp.bfloat16)
    keys = product(normed, wk).astype(jnp.bfloat16)
    values = (product(normed, wv) + bv.astype(jnp.float32)).astype(jnp.bfloat16)
    heads_q = query.reshape(count, HEADS, HEAD_DIM)
    heads_k = keys.reshape(count, HEADS, HEAD_DIM)
    heads_v = values.reshape(count, HEADS, HEAD_DIM)
    scores = masked_scores(heads_q, heads_k, allowed)
    peak = jnp.max(scores, axis=-1, keepdims=True)
    expo = jnp.exp(scores - peak)
    total = jnp.sum(expo, axis=-1, keepdims=True)
    logsum = peak + jnp.log(total)
    probs_low = (expo / total).astype(jnp.bfloat16)
    mixed = jnp.einsum("hqk,khd->qhd", probs_low, heads_v, preferred_element_type=jnp.float32)
    mixed = mixed.reshape(count, width).astype(jnp.bfloat16)
    middle = rows + product(mixed, wo) + bo.astype(jnp.float32)
    gain_second = gain_two.astype(jnp.float32)
    shift_second = shift_two.astype(jnp.float32)
    normed_two = layer_norm(middle, gain_second, shift_second).astype(jnp.bfloat16)
    hidden = product(normed_two, w_one) + b_one.astype(jnp.float32)
    active = gelu_exact(hidden).astype(jnp.bfloat16)
    result = (middle + product(active, w_two) + b_two.astype(jnp.float32)).astype(jnp.bfloat16)
    back_wq, back_wk, back_wv, back_wo = (wq, wk, wv, wo)
    back_w_one, back_w_two = (w_one, w_two)
    live = (seg_ids >= 0).astype(jnp.float32)[:, None]
    upstream = grad_out.astype(jnp.float32) * live
    grad_b_two = jnp.sum(upstream, axis=0)
    up_low = upstream.astype(jnp.bfloat16)
    grad_w_two = inner(active, up_low)
    grad_active = against(up_low, back_w_two)
    gelu_out, gelu_pull = jax.vjp(gelu_exact, hidden)
    grad_hidden = gelu_pull(grad_active)[0].astype(jnp.bfloat16)
    grad_b_one = column_sum(grad_hidden)
    grad_w_one = inner(normed_two, grad_hidden)
    grad_normed_two = against(grad_hidden, back_w_one)
    norm_out, norm_pull = jax.vjp(layer_norm, middle, gain_second, shift_second)
    grad_mid_norm, grad_gain_two, grad_shift_two = norm_pull(grad_normed_two)
    grad_middle = upstream + grad_mid_norm
    grad_bo = jnp.sum(grad_middle, axis=0)
    mid_low = grad_middle.astype(jnp.bfloat16)
    grad_wo = inner(mixed, mid_low)
    grad_mixed = against(mid_low, back_wo).astype(jnp.bfloat16).reshape(count, HEADS, HEAD_DIM)
    scores_again = masked_scores(heads_q, heads_k, allowed)
    probs = jnp.exp(scores_again - logsum)
    probs_again = probs.astype(jnp.bfloat16)
    grad_probs = jnp.einsum("qhd,khd->hqk", grad_mixed, heads_v, preferred_element_type=jnp.float32)
    grad_values = jnp.einsum(
        "hqk,qhd->khd", probs_again, grad_mixed, preferred_element_type=jnp.float32
    )
    grad_values = grad_values.reshape(count, width).astype(jnp.bfloat16)
    inner_sum = jnp.sum(grad_probs * probs, axis=-1, keepdims=True)
    grad_scores = (probs * (grad_probs - inner_sum) * HEAD_DIM ** (-0.5)).astype(jnp.bfloat16)
    grad_query = jnp.einsum(
        "hqk,khd->qhd", grad_scores, heads_k, preferred_element_type=jnp.float32
    )
    grad_query = grad_query.reshape(count, width).astype(jnp.bfloat16)
    grad_keys = jnp.einsum("hqk,qhd->khd", grad_scores, heads_q, preferred_element_type=jnp.float32)
    grad_keys = grad_keys.reshape(count, width).astype(jnp.bfloat16)
    grad_bq = column_sum(grad_query)
    grad_bv = column_sum(grad_values)
    grad_wq = inner(normed, grad_query)
    grad_wk = inner(normed, grad_keys)
    grad_wv = inner(normed, grad_values)
    grad_normed = (
        against(grad_query, back_wq) + against(grad_keys, back_wk) + against(grad_values, back_wv)
    )
    first_out, first_pull = jax.vjp(layer_norm, rows, gain_first, shift_first)
    grad_rows_norm, grad_gain_one, grad_shift_one = first_pull(grad_normed)
    grad_input = grad_middle + grad_rows_norm
    return result, grad_input, (
        grad_gain_one,
        grad_shift_one,
        grad_wq,
        grad_wk,
        grad_wv,
        grad_bq,
        grad_bv,
        grad_wo,
        grad_bo,
        grad_gain_two,
        grad_shift_two,
        grad_w_one,
        grad_b_one,
        grad_w_two,
        grad_b_two,
    )


def on_device_plain(tokens, seg_ids, grad_out, *params):
    gathered = tuple(lax.all_gather(p, "shard", axis=0, tiled=True) for p in params)
    result, grad_input, grads = layer(tokens, seg_ids, grad_out, gathered)
    owned = tuple(
        lax.psum_scatter(g, "shard", scatter_dimension=0, tiled=True) for g in grads
    )
    owned = lax.psum(owned, "rep")
    return (result, grad_input) + owned


HALVES = 2
THIRDS = 3
MESH = pl.DeviceIdType.MESH


def place():
    rep, shard = lax.axis_index("rep"), lax.axis_index("shard")
    return rep // 2, rep % 2, shard // 2, shard % 2


def device(y, core, z, x):
    return (2 * y + core, 2 * z + x)


def greet(y, core, z, x):
    barrier = pltpu.get_barrier_semaphore()
    peers = [
        device(y, 1 - core, z, x),
        device(1 - y, core, z, x),
        device(y, core, z, 1 - x),
    ] + [device(y, core, (z + d) % 4, x) for d in (1, 2, 3)]
    for peer in peers:
        pl.semaphore_signal(barrier, inc=1, device_id=peer, device_id_type=MESH)
    pl.semaphore_wait(barrier, len(peers))


def remote(src, dst, send_sem, recv_sem, peer):
    return pltpu.make_async_remote_copy(
        src_ref=src,
        dst_ref=dst,
        send_sem=send_sem,
        recv_sem=recv_sem,
        device_id=peer,
        device_id_type=MESH,
    )


def cut(shapes, limit):
    pieces = []
    for at, (rows, cols) in enumerate(shapes):
        if rows * cols <= limit:
            pieces.append((at, 0, rows, 0, cols))
        elif rows > 16:
            step = max(16, limit // cols // 16 * 16)
            pieces += [(at, r, step, 0, cols) for r in range(0, rows, step)]
        else:
            step = limit // rows // 128 * 128
            pieces += [(at, 0, rows, c, step) for c in range(0, cols, step)]
    return pieces


def gather_kernel(pieces, count, *refs):
    ins, outs = refs[:count], refs[count : 2 * count]
    own_sem, zs, zr, xs, xr, ys, yr, cs, cr = refs[2 * count :]
    y, core, z, x = place()
    total = len(pieces)

    def part(ref, piece, *lead):
        _, r, rows, c, cols = piece
        return ref.at[(*lead, pl.ds(r, rows), pl.ds(c, cols))]

    own = []
    for a, piece in enumerate(pieces):
        own.append(
            pltpu.make_async_copy(
                part(ins[piece[0]], piece, core, pl.ds(y, 2)),
                part(outs[piece[0]], piece, z, x, core, pl.ds(y, 2)),
                own_sem.at[a],
            )
        )
        own[a].start()
    greet(y, core, z, x)
    by_z, by_x, by_y, by_core = [], [], [], []
    for a, piece in enumerate(pieces):
        out = outs[piece[0]]
        by_z.append(
            [
                remote(
                    part(ins[piece[0]], piece, core, pl.ds(y, 2)),
                    part(out, piece, z, x, core, pl.ds(y, 2)),
                    zs.at[a, d - 1],
                    zr.at[a, d - 1],
                    device(y, core, (z + d) % 4, x),
                )
                for d in (1, 2, 3)
            ]
        )
        ref = part(out, piece, slice(None), x, core, pl.ds(y, 2))
        by_x.append(remote(ref, ref, xs.at[a], xr.at[a], device(y, core, z, 1 - x)))
        ref = part(out, piece, slice(None), slice(None), core, 2 * y)
        by_y.append(remote(ref, ref, ys.at[a], yr.at[a], device(1 - y, core, z, x)))
        ref = part(out, piece, slice(None), slice(None), core, slice(None))
        by_core.append(remote(ref, ref, cs.at[a], cr.at[a], device(y, 1 - core, z, x)))
    for copies in by_z:
        for copy in copies:
            copy.start()
    for step in range(total + 2):
        if 0 <= step - 2 < total:
            by_y[step - 2].wait_recv()
            by_core[step - 2].start()
        if 0 <= step - 1 < total:
            by_x[step - 1].wait_recv()
            by_y[step - 1].start()
        if step < total:
            own[step].wait()
            for copy in by_z[step]:
                copy.wait_recv()
            by_x[step].start()
    for a in range(total):
        by_core[a].wait_recv()
    for a in range(total):
        for copy in by_z[a]:
            copy.wait_send()
        by_x[a].wait_send()
        by_y[a].wait_send()
        by_core[a].wait_send()


def gather_all(shards):
    shapes = [s.shape[2:] for s in shards]
    pieces = cut(shapes, 16 * 1536)
    total, count = len(pieces), len(shards)
    dma = pltpu.SemaphoreType.DMA
    return pl.pallas_call(
        functools.partial(gather_kernel, pieces, count),
        out_shape=[jax.ShapeDtypeStruct((4, 2) + s.shape, s.dtype) for s in shards],
        in_specs=[pl.BlockSpec(memory_space=pl.ANY)] * count,
        out_specs=[pl.BlockSpec(memory_space=pl.ANY)] * count,
        scratch_shapes=[
            dma((total,)),
            dma((total, 3)),
            dma((total, 3)),
        ]
        + [dma((total,))] * 6,
        compiler_params=pltpu.CompilerParams(collective_id=0, has_side_effects=True),
        name="gather_parameters",
    )(*shards)


def reduce_kernel(pieces, count, *refs):
    ins, outs = refs[:count], refs[count : 2 * count]
    total = len(pieces)
    bufs = refs[2 * count : 2 * count + 5 * total]
    one, two, three, four, five = [bufs[i * total : (i + 1) * total] for i in range(5)]
    done = refs[2 * count + 5 * total : 2 * count + 6 * total]
    sems = refs[2 * count + 6 * total :]
    cs, cr, ys, yr, xs, xr, zs, zr, us, ur, fs, fr = sems
    y, core, z, x = place()
    f32, b16 = jnp.float32, jnp.bfloat16

    def part(ref, piece, *lead):
        _, r, rows, c, cols = piece
        return ref.at[(*lead, pl.ds(r, rows), pl.ds(c, cols))]

    every = slice(None)
    by_core, by_y, by_x, by_z, back_y, back_core = [], [], [], [], [], []
    for a, piece in enumerate(pieces):
        by_core.append(
            remote(
                part(ins[piece[0]], piece, every, every, 1 - core, every),
                one[a],
                cs.at[a],
                cr.at[a],
                device(y, 1 - core, z, x),
            )
        )
        by_y.append(
            remote(
                one[a].at[:, :, 2 * (1 - y)],
                two[a],
                ys.at[a],
                yr.at[a],
                device(1 - y, core, z, x),
            )
        )
        by_x.append(
            remote(
                one[a].at[:, 1 - x, pl.ds(y, 2)],
                three[a],
                xs.at[a],
                xr.at[a],
                device(y, core, z, 1 - x),
            )
        )
        by_z.append(
            [
                remote(
                    three[a].at[(z + d) % 4],
                    four[a].at[d - 1],
                    zs.at[a, d - 1],
                    zr.at[a, d - 1],
                    device(y, core, (z + d) % 4, x),
                )
                for d in (1, 2, 3)
            ]
        )
        back_y.append(
            remote(done[a], five[a], us.at[a], ur.at[a], device(1 - y, core, z, x))
        )
        final = part(outs[piece[0]], piece, core, every)
        back_core.append(
            remote(final, final, fs.at[a], fr.at[a], device(y, 1 - core, z, x))
        )

    def add_core(a):
        by_core[a].wait_recv()
        mine = part(ins[pieces[a][0]], pieces[a], every, every, core, every)

        @pl.loop(0, 8)
        def _(s):
            i, j = s // 2, s % 2
            one[a][i, j] = (one[a][i, j].astype(f32) + mine[i, j].astype(f32)).astype(b16)

        by_y[a].start()

    def add_y(a):
        by_y[a].wait_recv()

        @pl.loop(0, 8)
        def _(s):
            i, j = s // 2, s % 2
            one[a][i, j, 2 * y] = (
                one[a][i, j, 2 * y].astype(f32) + two[a][i, j].astype(f32)
            ).astype(b16)

        by_x[a].start()

    def add_x(a):
        by_x[a].wait_recv()

        @pl.loop(0, 4)
        def _(i):
            three[a][i] = (
                three[a][i].astype(f32) + one[a][i, x, pl.ds(y, 2)].astype(f32)
            ).astype(b16)

        for copy in by_z[a]:
            copy.start()

    def add_z(a):
        for copy in by_z[a]:
            copy.wait_recv()
        done[a][...] = (
            (three[a][z].astype(f32) + four[a][0].astype(f32))
            + (four[a][1].astype(f32) + four[a][2].astype(f32))
        ).astype(b16)
        back_y[a].start()

    def add_planes(a):
        back_y[a].wait_recv()
        out = part(outs[pieces[a][0]], pieces[a], core, every)
        out[1] = (done[a][1 - y].astype(f32) + five[a][y].astype(f32)).astype(b16)
        out[2 * y] = done[a][y]
        out[2 * (1 - y)] = five[a][1 - y]
        back_core[a].start()

    greet(y, core, z, x)
    for a in range(total):
        by_core[a].start()
    stages = (add_core, add_y, add_x, add_z, add_planes)
    for step in range(total + len(stages) - 1):
        for late in reversed(range(len(stages))):
            if 0 <= step - late < total:
                stages[late](step - late)
    for a in range(total):
        back_core[a].wait_recv()
    for a in range(total):
        by_core[a].wait_send()
        by_y[a].wait_send()
        by_x[a].wait_send()
        for copy in by_z[a]:
            copy.wait_send()
        back_y[a].wait_send()
        back_core[a].wait_send()


def reduce_all(grads):
    shapes = [g.shape[4:] for g in grads]
    pieces = cut(shapes, 16 * 1536)
    total, count = len(pieces), len(grads)
    dma = pltpu.SemaphoreType.DMA
    leads = ((4, 2, 3), (4, 2), (4, 2), (3, 2), (2,), (2,))
    buffers = [
        pltpu.VMEM(lead + (p[2], p[4]), jnp.bfloat16) for lead in leads for p in pieces
    ]
    single, triple = dma((total,)), dma((total, 3))
    return pl.pallas_call(
        functools.partial(reduce_kernel, pieces, count),
        out_shape=[jax.ShapeDtypeStruct(g.shape[2:], g.dtype) for g in grads],
        in_specs=[pl.BlockSpec(memory_space=pltpu.VMEM)] * count,
        out_specs=[pl.BlockSpec(memory_space=pltpu.VMEM)] * count,
        scratch_shapes=buffers + [single] * 6 + [triple] * 2 + [single] * 4,
        compiler_params=pltpu.CompilerParams(
            collective_id=1, has_side_effects=True, vmem_limit_bytes=52 * 1024 * 1024
        ),
        name="reduce_gradients",
    )(*grads)


VECTORS = (0, 1, 5, 6, 8, 9, 10, 14)
MATRICES = (2, 3, 4, 7, 11, 13)
B_ONE = 12


def on_device(tokens, seg_ids, grad_out, *params):
    width = params[0].shape[0]
    lanes = 128
    rows = 96

    def folded(w):
        return w.reshape(HALVES, THIRDS, w.shape[0] // 6, w.shape[1])

    small = jnp.concatenate(
        [jnp.pad(params[i][None], ((0, 0), (0, lanes - width))) for i in VECTORS]
        + [params[B_ONE].reshape(-1, lanes)]
    )
    small = jnp.pad(small, ((0, rows - small.shape[0]), (0, 0)))
    whole = gather_all([folded(small)] + [folded(params[i]) for i in MATRICES])
    gathered = [None] * len(params)
    small = whole[0].reshape(8, rows, lanes)
    for at, i in enumerate(VECTORS):
        gathered[i] = small[:, at, :width].reshape(-1)
    many = params[B_ONE].shape[0] // lanes
    gathered[B_ONE] = small[:, len(VECTORS) : len(VECTORS) + many].reshape(-1)
    for at, i in enumerate(MATRICES):
        gathered[i] = whole[1 + at].reshape(-1, params[i].shape[1])

    result, grad_input, grads = layer(tokens, seg_ids, grad_out, gathered)

    low = [g.astype(jnp.bfloat16) for g in grads]
    vectors = jnp.stack([low[i].reshape(8, width) for i in VECTORS], axis=1)
    vectors = jnp.pad(vectors, ((0, 0), (0, 0), (0, lanes - width)))
    vectors = jnp.concatenate([vectors, low[B_ONE].reshape(8, many, lanes)], axis=1)
    vectors = jnp.pad(vectors, ((0, 0), (0, rows - vectors.shape[1]), (0, 0)))
    shapes = [(rows, lanes)] + [params[i].shape for i in MATRICES]
    arrays = [vectors] + [low[i] for i in MATRICES]
    sums = reduce_all(
        [
            g.reshape(4, 2, HALVES, THIRDS, shape[0] // 6, shape[1])
            for g, shape in zip(arrays, shapes)
        ]
    )
    sums = [s.reshape(shape).astype(jnp.float32) for s, shape in zip(sums, shapes)]
    owned = [None] * len(params)
    for at, i in enumerate(VECTORS):
        owned[i] = sums[0][at, :width]
    owned[B_ONE] = sums[0][len(VECTORS) : len(VECTORS) + many].reshape(-1)
    for at, i in enumerate(MATRICES):
        owned[i] = sums[1 + at]
    return (result, grad_input) + tuple(owned)


def solution(mesh):
    in_specs = (
        P(("rep", "shard"), None),
        P(("rep", "shard")),
        P(("rep", "shard"), None),
        P("shard"),
        P("shard"),
        P("shard", None),
        P("shard", None),
        P("shard", None),
        P("shard"),
        P("shard"),
        P("shard", None),
        P("shard"),
        P("shard"),
        P("shard"),
        P("shard", None),
        P("shard"),
        P("shard", None),
        P("shard"),
    )
    out_specs = (
        P(("rep", "shard"), None),
        P(("rep", "shard"), None),
        P("shard"),
        P("shard"),
        P("shard", None),
        P("shard", None),
        P("shard", None),
        P("shard"),
        P("shard"),
        P("shard", None),
        P("shard"),
        P("shard"),
        P("shard"),
        P("shard", None),
        P("shard"),
        P("shard", None),
        P("shard"),
    )
    shape = dict(mesh.shape)
    fits = shape["rep"] == 4 and shape["shard"] == 8
    return jax.shard_map(
        on_device if fits else on_device_plain, mesh=mesh, in_specs=in_specs, out_specs=out_specs, check_vma=False
    )
```

```python
import functools

import jax
import jax.numpy as jnp
from jax import lax
from jax.experimental import pallas as pl
from jax.experimental.pallas import tpu as pltpu
from jax.sharding import PartitionSpec as P

HEADS = 12
HEAD_DIM = 64


norm_eps = 1e-05


def layer_norm(rows, gain, shift):
    center = rows - jnp.mean(rows, axis=-1, keepdims=True)
    spread = jnp.mean(center * center, axis=-1, keepdims=True)
    return center * lax.rsqrt(spread + norm_eps) * gain + shift


def gelu_exact(values):
    return jax.nn.gelu(values, approximate=False)


def product(left, right):
    return jnp.dot(left, right, preferred_element_type=jnp.float32)


def inner(left, right):
    return lax.dot_general(
        left, right, (((0,), (0,)), ((), ())), preferred_element_type=jnp.float32
    )


def against(left, right):
    return lax.dot_general(
        left, right, (((1,), (1,)), ((), ())), preferred_element_type=jnp.float32
    )


def column_sum(values):
    return jnp.sum(values.astype(jnp.float32), axis=0)


def head_probs(query, keys, allowed):
    scores = against(query, keys) * HEAD_DIM ** (-0.5)
    scores = jnp.where(allowed, scores, -1e30)
    expo = jnp.exp(scores - jnp.max(scores, axis=-1, keepdims=True))
    return expo / jnp.sum(expo, axis=-1, keepdims=True)


def allowed_pairs(seg_col, seg_row):
    count = seg_col.shape[0]
    row = lax.broadcasted_iota(jnp.int32, (count, count), 0)
    col = lax.broadcasted_iota(jnp.int32, (count, count), 1)
    return (seg_col[...] == seg_row[...]) & (row >= col)


def attend_kernel(seg_col, seg_row, query, keys, values, mixed):
    allowed = allowed_pairs(seg_col, seg_row)
    for first in range(0, HEADS, 2):
        parts = []
        for head in (first, first + 1):
            at = slice(head * HEAD_DIM, (head + 1) * HEAD_DIM)
            probs = head_probs(query[:, at], keys[:, at], allowed)
            parts.append(product(probs.astype(jnp.bfloat16), values[:, at]))
        at = slice(first * HEAD_DIM, (first + 2) * HEAD_DIM)
        mixed[:, at] = jnp.concatenate(parts, axis=1).astype(jnp.bfloat16)


def attend_back_kernel(
    seg_col, seg_row, query, keys, values, grad_mixed, grad_query, grad_keys, grad_values
):
    allowed = allowed_pairs(seg_col, seg_row)
    for first in range(0, HEADS, 2):
        parts = []
        for head in (first, first + 1):
            at = slice(head * HEAD_DIM, (head + 1) * HEAD_DIM)
            q, k, v, g = query[:, at], keys[:, at], values[:, at], grad_mixed[:, at]
            probs = head_probs(q, k, allowed)
            grad_probs = against(g, v)
            inner_sum = jnp.sum(grad_probs * probs, axis=-1, keepdims=True)
            grad_scores = (probs * (grad_probs - inner_sum) * HEAD_DIM ** (-0.5)).astype(
                jnp.bfloat16
            )
            parts.append(
                (
                    product(grad_scores, k),
                    inner(grad_scores, q),
                    inner(probs.astype(jnp.bfloat16), g),
                )
            )
        at = slice(first * HEAD_DIM, (first + 2) * HEAD_DIM)
        for ref, left, right in zip((grad_query, grad_keys, grad_values), *parts):
            ref[:, at] = jnp.concatenate([left, right], axis=1).astype(jnp.bfloat16)


def local_call(kernel, outputs, seg_ids, *arrays):
    vmem = pl.BlockSpec(memory_space=pltpu.VMEM)
    return pl.pallas_call(
        kernel,
        out_shape=[jax.ShapeDtypeStruct(arrays[0].shape, jnp.bfloat16)] * outputs,
        in_specs=[vmem] * (2 + len(arrays)),
        out_specs=[vmem] * outputs,
        compiler_params=pltpu.CompilerParams(vmem_limit_bytes=32 * 1024 * 1024),
    )(seg_ids[:, None], seg_ids[None, :], *arrays)


def layer(tokens, seg_ids, grad_out, gathered):
    (
        gain_one,
        shift_one,
        wq,
        wk,
        wv,
        bq,
        bv,
        wo,
        bo,
        gain_two,
        shift_two,
        w_one,
        b_one,
        w_two,
        b_two,
    ) = gathered
    rows = tokens.astype(jnp.float32)
    gain_first = gain_one.astype(jnp.float32)
    shift_first = shift_one.astype(jnp.float32)
    normed = layer_norm(rows, gain_first, shift_first).astype(jnp.bfloat16)
    query = (product(normed, wq) + bq.astype(jnp.float32)).astype(jnp.bfloat16)
    keys = product(normed, wk).astype(jnp.bfloat16)
    values = (product(normed, wv) + bv.astype(jnp.float32)).astype(jnp.bfloat16)
    (mixed,) = local_call(attend_kernel, 1, seg_ids, query, keys, values)
    middle = rows + product(mixed, wo) + bo.astype(jnp.float32)
    gain_second = gain_two.astype(jnp.float32)
    shift_second = shift_two.astype(jnp.float32)
    normed_two = layer_norm(middle, gain_second, shift_second).astype(jnp.bfloat16)
    hidden = product(normed_two, w_one) + b_one.astype(jnp.float32)
    active = gelu_exact(hidden).astype(jnp.bfloat16)
    result = (middle + product(active, w_two) + b_two.astype(jnp.float32)).astype(jnp.bfloat16)
    back_wq, back_wk, back_wv, back_wo = (wq, wk, wv, wo)
    back_w_one, back_w_two = (w_one, w_two)
    live = (seg_ids >= 0).astype(jnp.float32)[:, None]
    upstream = grad_out.astype(jnp.float32) * live
    grad_b_two = jnp.sum(upstream, axis=0)
    up_low = upstream.astype(jnp.bfloat16)
    grad_w_two = (active, up_low)
    grad_active = against(up_low, back_w_two)
    gelu_out, gelu_pull = jax.vjp(gelu_exact, hidden)
    grad_hidden = gelu_pull(grad_active)[0].astype(jnp.bfloat16)
    grad_b_one = column_sum(grad_hidden)
    grad_w_one = (normed_two, grad_hidden)
    grad_normed_two = against(grad_hidden, back_w_one)
    norm_out, norm_pull = jax.vjp(layer_norm, middle, gain_second, shift_second)
    grad_mid_norm, grad_gain_two, grad_shift_two = norm_pull(grad_normed_two)
    grad_middle = upstream + grad_mid_norm
    grad_bo = jnp.sum(grad_middle, axis=0)
    mid_low = grad_middle.astype(jnp.bfloat16)
    grad_wo = (mixed, mid_low)
    grad_mixed = against(mid_low, back_wo).astype(jnp.bfloat16)
    grad_query, grad_keys, grad_values = local_call(
        attend_back_kernel, 3, seg_ids, query, keys, values, grad_mixed
    )
    grad_bq = column_sum(grad_query)
    grad_bv = column_sum(grad_values)
    grad_wq = (normed, grad_query)
    grad_wk = (normed, grad_keys)
    grad_wv = (normed, grad_values)
    grad_normed = (
        against(grad_query, back_wq) + against(grad_keys, back_wk) + against(grad_values, back_wv)
    )
    first_out, first_pull = jax.vjp(layer_norm, rows, gain_first, shift_first)
    grad_rows_norm, grad_gain_one, grad_shift_one = first_pull(grad_normed)
    grad_input = grad_middle + grad_rows_norm
    return result, grad_input, (
        grad_gain_one,
        grad_shift_one,
        grad_wq,
        grad_wk,
        grad_wv,
        grad_bq,
        grad_bv,
        grad_wo,
        grad_bo,
        grad_gain_two,
        grad_shift_two,
        grad_w_one,
        grad_b_one,
        grad_w_two,
        grad_b_two,
    )


def on_device_plain(tokens, seg_ids, grad_out, *params):
    gathered = tuple(lax.all_gather(p, "shard", axis=0, tiled=True) for p in params)
    result, grad_input, grads = layer(tokens, seg_ids, grad_out, gathered)
    grads = tuple(inner(*g) if isinstance(g, tuple) else g for g in grads)
    owned = tuple(
        lax.psum_scatter(g, "shard", scatter_dimension=0, tiled=True) for g in grads
    )
    owned = lax.psum(owned, "rep")
    return (result, grad_input) + owned


HALVES = 2
THIRDS = 3
MESH = pl.DeviceIdType.MESH
GATHER_PIECE, GATHER_AHEAD, GATHER_LAGS = 16 * 768, 4, (2, 4)
REDUCE_LAGS = (0, 2, 4, 6, 8, 10)


def place():
    rep, shard = lax.axis_index("rep"), lax.axis_index("shard")
    return rep // 2, rep % 2, shard // 2, shard % 2


def device(y, core, z, x):
    return (2 * y + core, 2 * z + x)


def greet(y, core, z, x):
    barrier = pltpu.get_barrier_semaphore()
    peers = [
        device(y, 1 - core, z, x),
        device(1 - y, core, z, x),
        device(y, core, z, 1 - x),
    ] + [device(y, core, (z + d) % 4, x) for d in (1, 2, 3)]
    for peer in peers:
        pl.semaphore_signal(barrier, inc=1, device_id=peer, device_id_type=MESH)
    pl.semaphore_wait(barrier, len(peers))


def remote(src, dst, send_sem, recv_sem, peer):
    return pltpu.make_async_remote_copy(
        src_ref=src,
        dst_ref=dst,
        send_sem=send_sem,
        recv_sem=recv_sem,
        device_id=peer,
        device_id_type=MESH,
    )


def cut(shapes, limit):
    pieces = []
    for at, (rows, cols) in enumerate(shapes):
        if rows * cols <= limit:
            pieces.append((at, 0, rows, 0, cols))
        elif rows > 16:
            step = max(16, limit // cols // 16 * 16)
            pieces += [(at, r, step, 0, cols) for r in range(0, rows, step)]
        else:
            step = limit // rows // 128 * 128
            pieces += [(at, 0, rows, c, step) for c in range(0, cols, step)]
    return pieces


def gather_kernel(pieces, count, *refs):
    ins, outs = refs[:count], refs[count : 2 * count]
    own_sem, zs, zr, xs, xr, ys, yr, cs, cr = refs[2 * count :]
    y, core, z, x = place()
    total = len(pieces)

    def part(ref, piece, *lead):
        _, r, rows, c, cols = piece
        return ref.at[(*lead, pl.ds(r, rows), pl.ds(c, cols))]

    own = []
    for a, piece in enumerate(pieces):
        own.append(
            pltpu.make_async_copy(
                part(ins[piece[0]], piece, core, pl.ds(y, 2)),
                part(outs[piece[0]], piece, z, x, core, pl.ds(y, 2)),
                own_sem.at[a],
            )
        )
        own[a].start()
    greet(y, core, z, x)
    by_z, by_x, by_y, by_core = [], [], [], []
    for a, piece in enumerate(pieces):
        out = outs[piece[0]]
        by_z.append(
            [
                remote(
                    part(ins[piece[0]], piece, core, pl.ds(y, 2)),
                    part(out, piece, z, x, core, pl.ds(y, 2)),
                    zs.at[a, d - 1],
                    zr.at[a, d - 1],
                    device(y, core, (z + d) % 4, x),
                )
                for d in (1, 2, 3)
            ]
        )
        ref = part(out, piece, slice(None), x, core, pl.ds(y, 2))
        by_x.append(remote(ref, ref, xs.at[a], xr.at[a], device(y, core, z, 1 - x)))
        ref = part(out, piece, slice(None), slice(None), core, 2 * y)
        by_y.append(remote(ref, ref, ys.at[a], yr.at[a], device(1 - y, core, z, x)))
        ref = part(out, piece, slice(None), slice(None), core, slice(None))
        by_core.append(remote(ref, ref, cs.at[a], cr.at[a], device(y, 1 - core, z, x)))
    for copies in by_z[:GATHER_AHEAD]:
        for copy in copies:
            copy.start()
    x_lag, y_lag = GATHER_LAGS
    for step in range(total + y_lag):
        if 0 <= step - y_lag < total:
            by_y[step - y_lag].wait_recv()
            by_core[step - y_lag].start()
        if 0 <= step - x_lag < total:
            by_x[step - x_lag].wait_recv()
            by_y[step - x_lag].start()
        if step < total:
            own[step].wait()
            for copy in by_z[step]:
                copy.wait_recv()
            by_x[step].start()
            if step + GATHER_AHEAD < total:
                for copy in by_z[step + GATHER_AHEAD]:
                    copy.start()
    for a in range(total):
        by_core[a].wait_recv()
    for a in range(total):
        for copy in by_z[a]:
            copy.wait_send()
        by_x[a].wait_send()
        by_y[a].wait_send()
        by_core[a].wait_send()


def gather_all(shards):
    shapes = [s.shape[2:] for s in shards]
    pieces = cut(shapes, GATHER_PIECE)
    total, count = len(pieces), len(shards)
    dma = pltpu.SemaphoreType.DMA
    return pl.pallas_call(
        functools.partial(gather_kernel, pieces, count),
        out_shape=[jax.ShapeDtypeStruct((4, 2) + s.shape, s.dtype) for s in shards],
        in_specs=[pl.BlockSpec(memory_space=pl.ANY)] * count,
        out_specs=[pl.BlockSpec(memory_space=pl.ANY)] * count,
        scratch_shapes=[
            dma((total,)),
            dma((total, 3)),
            dma((total, 3)),
        ]
        + [dma((total,))] * 6,
        compiler_params=pltpu.CompilerParams(collective_id=0, has_side_effects=True),
        name="gather_parameters",
    )(*shards)


def reduce_kernel(pieces, factors, operands, small, *refs):
    ins, outs = refs[:operands], refs[operands : operands + len(factors) + 1]
    total = len(pieces)
    bufs = refs[operands + len(factors) + 1 :]
    sems = bufs[7 * total :]
    terms, one, two, three, four, five, done = [
        bufs[i * total : (i + 1) * total] for i in range(7)
    ]
    cs, cr, ys, yr, xs, xr, zs, zr, us, ur, fs, fr = sems
    y, core, z, x = place()
    f32, b16 = jnp.float32, jnp.bfloat16

    def part(ref, piece, *lead):
        _, r, rows, c, cols = piece
        return ref.at[(*lead, pl.ds(r, rows), pl.ds(c, cols))]

    every = slice(None)
    by_core, by_y, by_x, by_z, back_y, back_core = [], [], [], [], [], []
    for a, piece in enumerate(pieces):
        by_core.append(
            remote(
                terms[a].at[:, :, 1 - core],
                one[a],
                cs.at[a],
                cr.at[a],
                device(y, 1 - core, z, x),
            )
        )
        by_y.append(
            remote(
                one[a].at[:, :, 2 * (1 - y)],
                two[a],
                ys.at[a],
                yr.at[a],
                device(1 - y, core, z, x),
            )
        )
        by_x.append(
            remote(
                one[a].at[:, 1 - x, pl.ds(y, 2)],
                three[a],
                xs.at[a],
                xr.at[a],
                device(y, core, z, 1 - x),
            )
        )
        by_z.append(
            [
                remote(
                    three[a].at[(z + d) % 4],
                    four[a].at[d - 1],
                    zs.at[a, d - 1],
                    zr.at[a, d - 1],
                    device(y, core, (z + d) % 4, x),
                )
                for d in (1, 2, 3)
            ]
        )
        back_y.append(
            remote(done[a], five[a], us.at[a], ur.at[a], device(1 - y, core, z, x))
        )
        final = part(outs[piece[0]], piece, core, every)
        back_core.append(
            remote(final, final, fs.at[a], fr.at[a], device(y, 1 - core, z, x))
        )

    def make(a):
        at, _, _, c, cols = pieces[a]
        if at == 0:
            terms[a][...] = small[...]
        else:
            left, right = factors[at - 1]
            term = lax.dot_general(
                ins[left][...],
                ins[right][:, c : c + cols],
                (((0,), (0,)), ((), ())),
                preferred_element_type=f32,
            )
            terms[a][...] = term.reshape(terms[a].shape).astype(b16)
        by_core[a].start()

    def add_core(a):
        by_core[a].wait_recv()
        mine = terms[a].at[:, :, core]

        @pl.loop(0, 8)
        def _(s):
            i, j = s // 2, s % 2
            one[a][i, j] = (one[a][i, j].astype(f32) + mine[i, j].astype(f32)).astype(b16)

        by_y[a].start()

    def add_y(a):
        by_y[a].wait_recv()

        @pl.loop(0, 8)
        def _(s):
            i, j = s // 2, s % 2
            one[a][i, j, 2 * y] = (
                one[a][i, j, 2 * y].astype(f32) + two[a][i, j].astype(f32)
            ).astype(b16)

        by_x[a].start()

    def add_x(a):
        by_x[a].wait_recv()

        @pl.loop(0, 4)
        def _(i):
            three[a][i] = (
                three[a][i].astype(f32) + one[a][i, x, pl.ds(y, 2)].astype(f32)
            ).astype(b16)

        for copy in by_z[a]:
            copy.start()

    def add_z(a):
        for copy in by_z[a]:
            copy.wait_recv()
        done[a][...] = (
            (three[a][z].astype(f32) + four[a][0].astype(f32))
            + (four[a][1].astype(f32) + four[a][2].astype(f32))
        ).astype(b16)
        back_y[a].start()

    def add_planes(a):
        back_y[a].wait_recv()
        out = part(outs[pieces[a][0]], pieces[a], core, every)
        out[1] = (done[a][1 - y].astype(f32) + five[a][y].astype(f32)).astype(b16)
        out[2 * y] = done[a][y]
        out[2 * (1 - y)] = five[a][1 - y]
        back_core[a].start()

    greet(y, core, z, x)
    stages = (make, add_core, add_y, add_x, add_z, add_planes)
    for step in range(total + REDUCE_LAGS[-1]):
        for stage, lag in zip(reversed(stages), reversed(REDUCE_LAGS)):
            if 0 <= step - lag < total:
                stage(step - lag)
    for a in range(total):
        back_core[a].wait_recv()
    for a in range(total):
        by_core[a].wait_send()
        by_y[a].wait_send()
        by_x[a].wait_send()
        for copy in by_z[a]:
            copy.wait_send()
        back_y[a].wait_send()
        back_core[a].wait_send()


def reduce_all(small, pairs):
    operands, factors = [], []
    for pair in pairs:
        for value in pair:
            if not any(value is other for other in operands):
                operands.append(value)
        factors.append(
            tuple([value is other for other in operands].index(True) for value in pair)
        )
    shards = 8 * HALVES * THIRDS
    shapes = [small.shape[4:]] + [(l.shape[1] // shards, r.shape[1]) for l, r in pairs]
    pieces = []
    for at, (rows, cols) in enumerate(shapes):
        step = min(cols, 768 if rows == 16 else 256)
        pieces += [(at, 0, rows, c, step) for c in range(0, cols, step)]
    total = len(pieces)
    dma = pltpu.SemaphoreType.DMA
    leads = ((4, 2, HALVES, 3), (4, 2, 3), (4, 2), (4, 2), (3, 2), (2,), (2,))
    buffers = [
        pltpu.VMEM(lead + (p[2], p[4]), jnp.bfloat16) for lead in leads for p in pieces
    ]
    single, triple = dma((total,)), dma((total, 3))
    vmem = pl.BlockSpec(memory_space=pltpu.VMEM)

    def kernel(small_ref, *refs):
        reduce_kernel(pieces, factors, len(operands), small_ref, *refs)

    return pl.pallas_call(
        kernel,
        out_shape=[
            jax.ShapeDtypeStruct((HALVES, THIRDS) + shape, jnp.bfloat16) for shape in shapes
        ],
        in_specs=[vmem] * (1 + len(operands)),
        out_specs=[vmem] * len(shapes),
        scratch_shapes=buffers + [single] * 6 + [triple] * 2 + [single] * 4,
        compiler_params=pltpu.CompilerParams(
            collective_id=1, has_side_effects=True, vmem_limit_bytes=56 * 1024 * 1024
        ),
        name="reduce_gradients",
    )(small, *operands)


VECTORS = (0, 1, 5, 6, 8, 9, 10, 14)
MATRICES = (2, 3, 4, 7, 11, 13)
B_ONE = 12


def on_device(tokens, seg_ids, grad_out, *params):
    width = params[0].shape[0]
    lanes = 128
    rows = 96

    def folded(w):
        return w.reshape(HALVES, THIRDS, w.shape[0] // 6, w.shape[1])

    small = jnp.concatenate(
        [jnp.pad(params[i][None], ((0, 0), (0, lanes - width))) for i in VECTORS]
        + [params[B_ONE].reshape(-1, lanes)]
    )
    small = jnp.pad(small, ((0, rows - small.shape[0]), (0, 0)))
    whole = gather_all([folded(small)] + [folded(params[i]) for i in MATRICES])
    gathered = [None] * len(params)
    small = whole[0].reshape(8, rows, lanes)
    for at, i in enumerate(VECTORS):
        gathered[i] = small[:, at, :width].reshape(-1)
    many = params[B_ONE].shape[0] // lanes
    gathered[B_ONE] = small[:, len(VECTORS) : len(VECTORS) + many].reshape(-1)
    for at, i in enumerate(MATRICES):
        gathered[i] = whole[1 + at].reshape(-1, params[i].shape[1])

    result, grad_input, grads = layer(tokens, seg_ids, grad_out, gathered)

    low = {i: grads[i].astype(jnp.bfloat16) for i in VECTORS + (B_ONE,)}
    vectors = jnp.stack([low[i].reshape(8, width) for i in VECTORS], axis=1)
    vectors = jnp.pad(vectors, ((0, 0), (0, 0), (0, lanes - width)))
    vectors = jnp.concatenate([vectors, low[B_ONE].reshape(8, many, lanes)], axis=1)
    vectors = jnp.pad(vectors, ((0, 0), (0, rows - vectors.shape[1]), (0, 0)))
    shapes = [(rows, lanes)] + [params[i].shape for i in MATRICES]
    vectors = vectors.reshape(4, 2, HALVES, THIRDS, rows // 6, lanes)
    sums = reduce_all(vectors, [grads[i] for i in MATRICES])
    sums = [s.reshape(shape).astype(jnp.float32) for s, shape in zip(sums, shapes)]
    owned = [None] * len(params)
    for at, i in enumerate(VECTORS):
        owned[i] = sums[0][at, :width]
    owned[B_ONE] = sums[0][len(VECTORS) : len(VECTORS) + many].reshape(-1)
    for at, i in enumerate(MATRICES):
        owned[i] = sums[1 + at]
    return (result, grad_input) + tuple(owned)


def solution(mesh):
    in_specs = (
        P(("rep", "shard"), None),
        P(("rep", "shard")),
        P(("rep", "shard"), None),
        P("shard"),
        P("shard"),
        P("shard", None),
        P("shard", None),
        P("shard", None),
        P("shard"),
        P("shard"),
        P("shard", None),
        P("shard"),
        P("shard"),
        P("shard"),
        P("shard", None),
        P("shard"),
        P("shard", None),
        P("shard"),
    )
    out_specs = (
        P(("rep", "shard"), None),
        P(("rep", "shard"), None),
        P("shard"),
        P("shard"),
        P("shard", None),
        P("shard", None),
        P("shard", None),
        P("shard"),
        P("shard"),
        P("shard", None),
        P("shard"),
        P("shard"),
        P("shard"),
        P("shard", None),
        P("shard"),
        P("shard", None),
        P("shard"),
    )
    shape = dict(mesh.shape)
    fits = shape["rep"] == 4 and shape["shard"] == 8
    return jax.shard_map(
        on_device if fits else on_device_plain, mesh=mesh, in_specs=in_specs, out_specs=out_specs, check_vma=False
    )
```

```python
import functools

import jax
import jax.numpy as jnp
from jax import lax
from jax.experimental import pallas as pl
from jax.experimental.pallas import tpu as pltpu
from jax.sharding import PartitionSpec as P

HEADS = 12
HEAD_DIM = 64


norm_eps = 1e-05


def layer_norm(rows, gain, shift):
    center = rows - jnp.mean(rows, axis=-1, keepdims=True)
    spread = jnp.mean(center * center, axis=-1, keepdims=True)
    return center * lax.rsqrt(spread + norm_eps) * gain + shift


def gelu_exact(values):
    return jax.nn.gelu(values, approximate=False)


def product(left, right):
    return jnp.dot(left, right, preferred_element_type=jnp.float32)


def inner(left, right):
    return lax.dot_general(
        left, right, (((0,), (0,)), ((), ())), preferred_element_type=jnp.float32
    )


def against(left, right):
    return lax.dot_general(
        left, right, (((1,), (1,)), ((), ())), preferred_element_type=jnp.float32
    )


def column_sum(values):
    return jnp.sum(values.astype(jnp.float32), axis=0)


def head_probs(query, keys, allowed):
    scores = against(query, keys) * HEAD_DIM ** (-0.5)
    scores = jnp.where(allowed, scores, -1e30)
    expo = jnp.exp(scores - jnp.max(scores, axis=-1, keepdims=True))
    return expo / jnp.sum(expo, axis=-1, keepdims=True)


def allowed_pairs(seg_col, seg_row):
    count = seg_col.shape[0]
    row = lax.broadcasted_iota(jnp.int32, (count, count), 0)
    col = lax.broadcasted_iota(jnp.int32, (count, count), 1)
    return (seg_col[...] == seg_row[...]) & (row >= col)


def attend_kernel(seg_col, seg_row, query, keys, values, mixed):
    allowed = allowed_pairs(seg_col, seg_row)
    for first in range(0, HEADS, 2):
        parts = []
        for head in (first, first + 1):
            at = slice(head * HEAD_DIM, (head + 1) * HEAD_DIM)
            probs = head_probs(query[:, at], keys[:, at], allowed)
            parts.append(product(probs.astype(jnp.bfloat16), values[:, at]))
        at = slice(first * HEAD_DIM, (first + 2) * HEAD_DIM)
        mixed[:, at] = jnp.concatenate(parts, axis=1).astype(jnp.bfloat16)


def attend_back_kernel(
    seg_col, seg_row, query, keys, values, grad_mixed, grad_query, grad_keys, grad_values
):
    allowed = allowed_pairs(seg_col, seg_row)
    for first in range(0, HEADS, 2):
        parts = []
        for head in (first, first + 1):
            at = slice(head * HEAD_DIM, (head + 1) * HEAD_DIM)
            q, k, v, g = query[:, at], keys[:, at], values[:, at], grad_mixed[:, at]
            probs = head_probs(q, k, allowed)
            grad_probs = against(g, v)
            inner_sum = jnp.sum(grad_probs * probs, axis=-1, keepdims=True)
            grad_scores = (probs * (grad_probs - inner_sum) * HEAD_DIM ** (-0.5)).astype(
                jnp.bfloat16
            )
            parts.append(
                (
                    product(grad_scores, k),
                    inner(grad_scores, q),
                    inner(probs.astype(jnp.bfloat16), g),
                )
            )
        at = slice(first * HEAD_DIM, (first + 2) * HEAD_DIM)
        for ref, left, right in zip((grad_query, grad_keys, grad_values), *parts):
            ref[:, at] = jnp.concatenate([left, right], axis=1).astype(jnp.bfloat16)


def local_call(kernel, outputs, seg_ids, *arrays):
    vmem = pl.BlockSpec(memory_space=pltpu.VMEM)
    return pl.pallas_call(
        kernel,
        out_shape=[jax.ShapeDtypeStruct(arrays[0].shape, jnp.bfloat16)] * outputs,
        in_specs=[vmem] * (2 + len(arrays)),
        out_specs=[vmem] * outputs,
        compiler_params=pltpu.CompilerParams(vmem_limit_bytes=32 * 1024 * 1024),
    )(seg_ids[:, None], seg_ids[None, :], *arrays)


def layer(tokens, seg_ids, grad_out, gathered):
    (
        gain_one,
        shift_one,
        wq,
        wk,
        wv,
        bq,
        bv,
        wo,
        bo,
        gain_two,
        shift_two,
        w_one,
        b_one,
        w_two,
        b_two,
    ) = gathered
    rows = tokens.astype(jnp.float32)
    gain_first = gain_one.astype(jnp.float32)
    shift_first = shift_one.astype(jnp.float32)
    normed = layer_norm(rows, gain_first, shift_first).astype(jnp.bfloat16)
    query = (product(normed, wq) + bq.astype(jnp.float32)).astype(jnp.bfloat16)
    keys = product(normed, wk).astype(jnp.bfloat16)
    values = (product(normed, wv) + bv.astype(jnp.float32)).astype(jnp.bfloat16)
    (mixed,) = local_call(attend_kernel, 1, seg_ids, query, keys, values)
    middle = rows + product(mixed, wo) + bo.astype(jnp.float32)
    gain_second = gain_two.astype(jnp.float32)
    shift_second = shift_two.astype(jnp.float32)
    normed_two = layer_norm(middle, gain_second, shift_second).astype(jnp.bfloat16)
    hidden = product(normed_two, w_one) + b_one.astype(jnp.float32)
    active = gelu_exact(hidden).astype(jnp.bfloat16)
    result = (middle + product(active, w_two) + b_two.astype(jnp.float32)).astype(jnp.bfloat16)
    back_wq, back_wk, back_wv, back_wo = (wq, wk, wv, wo)
    back_w_one, back_w_two = (w_one, w_two)
    live = (seg_ids >= 0).astype(jnp.float32)[:, None]
    upstream = grad_out.astype(jnp.float32) * live
    grad_b_two = jnp.sum(upstream, axis=0)
    up_low = upstream.astype(jnp.bfloat16)
    grad_w_two = (active, up_low)
    grad_active = against(up_low, back_w_two)
    gelu_out, gelu_pull = jax.vjp(gelu_exact, hidden)
    grad_hidden = gelu_pull(grad_active)[0].astype(jnp.bfloat16)
    grad_b_one = column_sum(grad_hidden)
    grad_w_one = (normed_two, grad_hidden)
    grad_normed_two = against(grad_hidden, back_w_one)
    norm_out, norm_pull = jax.vjp(layer_norm, middle, gain_second, shift_second)
    grad_mid_norm, grad_gain_two, grad_shift_two = norm_pull(grad_normed_two)
    grad_middle = upstream + grad_mid_norm
    grad_bo = jnp.sum(grad_middle, axis=0)
    mid_low = grad_middle.astype(jnp.bfloat16)
    grad_wo = (mixed, mid_low)
    grad_mixed = against(mid_low, back_wo).astype(jnp.bfloat16)
    grad_query, grad_keys, grad_values = local_call(
        attend_back_kernel, 3, seg_ids, query, keys, values, grad_mixed
    )
    grad_bq = column_sum(grad_query)
    grad_bv = column_sum(grad_values)
    grad_wq = (normed, grad_query)
    grad_wk = (normed, grad_keys)
    grad_wv = (normed, grad_values)
    grad_normed = (
        against(grad_query, back_wq) + against(grad_keys, back_wk) + against(grad_values, back_wv)
    )
    first_out, first_pull = jax.vjp(layer_norm, rows, gain_first, shift_first)
    grad_rows_norm, grad_gain_one, grad_shift_one = first_pull(grad_normed)
    grad_input = grad_middle + grad_rows_norm
    return result, grad_input, (
        grad_gain_one,
        grad_shift_one,
        grad_wq,
        grad_wk,
        grad_wv,
        grad_bq,
        grad_bv,
        grad_wo,
        grad_bo,
        grad_gain_two,
        grad_shift_two,
        grad_w_one,
        grad_b_one,
        grad_w_two,
        grad_b_two,
    )


def on_device_plain(tokens, seg_ids, grad_out, *params):
    gathered = tuple(lax.all_gather(p, "shard", axis=0, tiled=True) for p in params)
    result, grad_input, grads = layer(tokens, seg_ids, grad_out, gathered)
    grads = tuple(inner(*g) if isinstance(g, tuple) else g for g in grads)
    owned = tuple(
        lax.psum_scatter(g, "shard", scatter_dimension=0, tiled=True) for g in grads
    )
    owned = lax.psum(owned, "rep")
    return (result, grad_input) + owned


HALVES = 2
THIRDS = 3
MESH = pl.DeviceIdType.MESH
GATHER_PIECE, GATHER_AHEAD, GATHER_LAGS = 16 * 768, 3, (2, 4)
REDUCE_LAGS = (0, 2, 5, 7, 9, 12)


def place():
    rep, shard = lax.axis_index("rep"), lax.axis_index("shard")
    return rep // 2, rep % 2, shard // 2, shard % 2


def device(y, core, z, x):
    return (2 * y + core, 2 * z + x)


def greet(y, core, z, x):
    barrier = pltpu.get_barrier_semaphore()
    peers = [
        device(y, 1 - core, z, x),
        device(1 - y, core, z, x),
        device(y, core, z, 1 - x),
    ] + [device(y, core, (z + d) % 4, x) for d in (1, 2, 3)]
    for peer in peers:
        pl.semaphore_signal(barrier, inc=1, device_id=peer, device_id_type=MESH)
    pl.semaphore_wait(barrier, len(peers))


def remote(src, dst, send_sem, recv_sem, peer):
    return pltpu.make_async_remote_copy(
        src_ref=src,
        dst_ref=dst,
        send_sem=send_sem,
        recv_sem=recv_sem,
        device_id=peer,
        device_id_type=MESH,
    )


def cut(shapes, limit):
    pieces = []
    for at, (rows, cols) in enumerate(shapes):
        if rows * cols <= limit:
            pieces.append((at, 0, rows, 0, cols))
        elif rows > 16:
            step = max(16, limit // cols // 16 * 16)
            pieces += [(at, r, step, 0, cols) for r in range(0, rows, step)]
        else:
            step = limit // rows // 128 * 128
            pieces += [(at, 0, rows, c, step) for c in range(0, cols, step)]
    return pieces


def gather_kernel(pieces, count, *refs):
    ins, outs = refs[:count], refs[count : 2 * count]
    own_sem, zs, zr, xs, xr, ys, yr, cs, cr = refs[2 * count :]
    y, core, z, x = place()
    total = len(pieces)

    def part(ref, piece, *lead):
        _, r, rows, c, cols = piece
        return ref.at[(*lead, pl.ds(r, rows), pl.ds(c, cols))]

    own = []
    for a, piece in enumerate(pieces):
        own.append(
            pltpu.make_async_copy(
                part(ins[piece[0]], piece, core, pl.ds(y, 2)),
                part(outs[piece[0]], piece, z, x, core, pl.ds(y, 2)),
                own_sem.at[a],
            )
        )
        own[a].start()
    greet(y, core, z, x)
    by_z, by_x, by_y, by_core = [], [], [], []
    for a, piece in enumerate(pieces):
        out = outs[piece[0]]
        by_z.append(
            [
                remote(
                    part(ins[piece[0]], piece, core, pl.ds(y, 2)),
                    part(out, piece, z, x, core, pl.ds(y, 2)),
                    zs.at[a, d - 1],
                    zr.at[a, d - 1],
                    device(y, core, (z + d) % 4, x),
                )
                for d in (1, 2, 3)
            ]
        )
        ref = part(out, piece, slice(None), x, core, pl.ds(y, 2))
        by_x.append(remote(ref, ref, xs.at[a], xr.at[a], device(y, core, z, 1 - x)))
        ref = part(out, piece, slice(None), slice(None), core, 2 * y)
        by_y.append(remote(ref, ref, ys.at[a], yr.at[a], device(1 - y, core, z, x)))
        ref = part(out, piece, slice(None), slice(None), core, slice(None))
        by_core.append(remote(ref, ref, cs.at[a], cr.at[a], device(y, 1 - core, z, x)))
    for copies in by_z[:GATHER_AHEAD]:
        for copy in copies:
            copy.start()
    x_lag, y_lag = GATHER_LAGS
    for step in range(total + y_lag):
        if 0 <= step - y_lag < total:
            by_y[step - y_lag].wait_recv()
            by_core[step - y_lag].start()
        if 0 <= step - x_lag < total:
            by_x[step - x_lag].wait_recv()
            by_y[step - x_lag].start()
        if step < total:
            own[step].wait()
            for copy in by_z[step]:
                copy.wait_recv()
            by_x[step].start()
            if step + GATHER_AHEAD < total:
                for copy in by_z[step + GATHER_AHEAD]:
                    copy.start()
    for a in range(total):
        by_core[a].wait_recv()
    for a in range(total):
        for copy in by_z[a]:
            copy.wait_send()
        by_x[a].wait_send()
        by_y[a].wait_send()
        by_core[a].wait_send()


def gather_all(shards):
    shapes = [s.shape[2:] for s in shards]
    pieces = cut(shapes, GATHER_PIECE)
    total, count = len(pieces), len(shards)
    dma = pltpu.SemaphoreType.DMA
    return pl.pallas_call(
        functools.partial(gather_kernel, pieces, count),
        out_shape=[jax.ShapeDtypeStruct((4, 2) + s.shape, s.dtype) for s in shards],
        in_specs=[pl.BlockSpec(memory_space=pl.ANY)] * count,
        out_specs=[pl.BlockSpec(memory_space=pl.ANY)] * count,
        scratch_shapes=[
            dma((total,)),
            dma((total, 3)),
            dma((total, 3)),
        ]
        + [dma((total,))] * 6,
        compiler_params=pltpu.CompilerParams(collective_id=0, has_side_effects=True),
        name="gather_parameters",
    )(*shards)


def reduce_kernel(pieces, factors, operands, small, *refs):
    ins, outs = refs[:operands], refs[operands : operands + len(factors) + 1]
    total = len(pieces)
    bufs = refs[operands + len(factors) + 1 :]
    sems = bufs[7 * total :]
    terms, one, two, three, four, five, done = [
        bufs[i * total : (i + 1) * total] for i in range(7)
    ]
    cs, cr, ys, yr, xs, xr, zs, zr, us, ur, fs, fr = sems
    y, core, z, x = place()
    f32, b16 = jnp.float32, jnp.bfloat16

    def part(ref, piece, *lead):
        _, r, rows, c, cols = piece
        return ref.at[(*lead, pl.ds(r, rows), pl.ds(c, cols))]

    every = slice(None)
    by_core, by_y, by_x, by_z, back_y, back_core = [], [], [], [], [], []
    for a, piece in enumerate(pieces):
        by_core.append(
            remote(
                terms[a].at[:, :, 1 - core],
                one[a],
                cs.at[a],
                cr.at[a],
                device(y, 1 - core, z, x),
            )
        )
        by_y.append(
            remote(
                one[a].at[:, :, 2 * (1 - y)],
                two[a],
                ys.at[a],
                yr.at[a],
                device(1 - y, core, z, x),
            )
        )
        by_x.append(
            remote(
                one[a].at[:, 1 - x, pl.ds(y, 2)],
                three[a],
                xs.at[a],
                xr.at[a],
                device(y, core, z, 1 - x),
            )
        )
        by_z.append(
            [
                remote(
                    three[a].at[(z + d) % 4],
                    four[a].at[d - 1],
                    zs.at[a, d - 1],
                    zr.at[a, d - 1],
                    device(y, core, (z + d) % 4, x),
                )
                for d in (1, 2, 3)
            ]
        )
        back_y.append(
            remote(done[a], five[a], us.at[a], ur.at[a], device(1 - y, core, z, x))
        )
        final = part(outs[piece[0]], piece, core, every)
        back_core.append(
            remote(final, final, fs.at[a], fr.at[a], device(y, 1 - core, z, x))
        )

    def make(a):
        at, _, _, c, cols = pieces[a]
        if at == 0:
            terms[a][...] = small[...]
        else:
            left, right = factors[at - 1]
            term = lax.dot_general(
                ins[left][...],
                ins[right][:, c : c + cols],
                (((0,), (0,)), ((), ())),
                preferred_element_type=f32,
            )
            terms[a][...] = term.reshape(terms[a].shape).astype(b16)
        by_core[a].start()

    def add_core(a):
        by_core[a].wait_recv()
        mine = terms[a].at[:, :, core]

        @pl.loop(0, 8)
        def _(s):
            i, j = s // 2, s % 2
            one[a][i, j] = (one[a][i, j].astype(f32) + mine[i, j].astype(f32)).astype(b16)

        by_y[a].start()

    def add_y(a):
        by_y[a].wait_recv()

        @pl.loop(0, 8)
        def _(s):
            i, j = s // 2, s % 2
            one[a][i, j, 2 * y] = (
                one[a][i, j, 2 * y].astype(f32) + two[a][i, j].astype(f32)
            ).astype(b16)

        by_x[a].start()

    def add_x(a):
        by_x[a].wait_recv()

        @pl.loop(0, 4)
        def _(i):
            three[a][i] = (
                three[a][i].astype(f32) + one[a][i, x, pl.ds(y, 2)].astype(f32)
            ).astype(b16)

        for copy in by_z[a]:
            copy.start()

    def add_z(a):
        for copy in by_z[a]:
            copy.wait_recv()
        done[a][...] = (
            (three[a][z].astype(f32) + four[a][0].astype(f32))
            + (four[a][1].astype(f32) + four[a][2].astype(f32))
        ).astype(b16)
        back_y[a].start()

    def add_planes(a):
        back_y[a].wait_recv()
        out = part(outs[pieces[a][0]], pieces[a], core, every)
        out[1] = (done[a][1 - y].astype(f32) + five[a][y].astype(f32)).astype(b16)
        out[2 * y] = done[a][y]
        out[2 * (1 - y)] = five[a][1 - y]
        back_core[a].start()

    greet(y, core, z, x)
    stages = (make, add_core, add_y, add_x, add_z, add_planes)
    for step in range(total + REDUCE_LAGS[-1]):
        for stage, lag in zip(reversed(stages), reversed(REDUCE_LAGS)):
            if 0 <= step - lag < total:
                stage(step - lag)
    for a in range(total):
        back_core[a].wait_recv()
    for a in range(total):
        by_core[a].wait_send()
        by_y[a].wait_send()
        by_x[a].wait_send()
        for copy in by_z[a]:
            copy.wait_send()
        back_y[a].wait_send()
        back_core[a].wait_send()


def reduce_all(small, pairs):
    operands, factors = [], []
    for pair in pairs:
        for value in pair:
            if not any(value is other for other in operands):
                operands.append(value)
        factors.append(
            tuple([value is other for other in operands].index(True) for value in pair)
        )
    shards = 8 * HALVES * THIRDS
    shapes = [small.shape[4:]] + [(l.shape[1] // shards, r.shape[1]) for l, r in pairs]
    pieces = []
    for at, (rows, cols) in enumerate(shapes):
        step = min(cols, 768 if rows == 16 else 256)
        pieces += [(at, 0, rows, c, step) for c in range(0, cols, step)]
    total = len(pieces)
    dma = pltpu.SemaphoreType.DMA
    leads = ((4, 2, HALVES, 3), (4, 2, 3), (4, 2), (4, 2), (3, 2), (2,), (2,))
    buffers = [
        pltpu.VMEM(lead + (p[2], p[4]), jnp.bfloat16) for lead in leads for p in pieces
    ]
    single, triple = dma((total,)), dma((total, 3))
    vmem = pl.BlockSpec(memory_space=pltpu.VMEM)

    def kernel(small_ref, *refs):
        reduce_kernel(pieces, factors, len(operands), small_ref, *refs)

    return pl.pallas_call(
        kernel,
        out_shape=[
            jax.ShapeDtypeStruct((HALVES, THIRDS) + shape, jnp.bfloat16) for shape in shapes
        ],
        in_specs=[vmem] * (1 + len(operands)),
        out_specs=[vmem] * len(shapes),
        scratch_shapes=buffers + [single] * 6 + [triple] * 2 + [single] * 4,
        compiler_params=pltpu.CompilerParams(
            collective_id=1, has_side_effects=True, vmem_limit_bytes=56 * 1024 * 1024
        ),
        name="reduce_gradients",
    )(small, *operands)


VECTORS = (0, 1, 5, 6, 8, 9, 10, 14)
MATRICES = (2, 3, 4, 7, 11, 13)
B_ONE = 12


def on_device(tokens, seg_ids, grad_out, *params):
    width = params[0].shape[0]
    lanes = 128
    rows = 96

    def folded(w):
        return w.reshape(HALVES, THIRDS, w.shape[0] // 6, w.shape[1])

    small = jnp.concatenate(
        [jnp.pad(params[i][None], ((0, 0), (0, lanes - width))) for i in VECTORS]
        + [params[B_ONE].reshape(-1, lanes)]
    )
    small = jnp.pad(small, ((0, rows - small.shape[0]), (0, 0)))
    whole = gather_all([folded(small)] + [folded(params[i]) for i in MATRICES])
    gathered = [None] * len(params)
    small = whole[0].reshape(8, rows, lanes)
    for at, i in enumerate(VECTORS):
        gathered[i] = small[:, at, :width].reshape(-1)
    many = params[B_ONE].shape[0] // lanes
    gathered[B_ONE] = small[:, len(VECTORS) : len(VECTORS) + many].reshape(-1)
    for at, i in enumerate(MATRICES):
        gathered[i] = whole[1 + at].reshape(-1, params[i].shape[1])

    result, grad_input, grads = layer(tokens, seg_ids, grad_out, gathered)

    low = {i: grads[i].astype(jnp.bfloat16) for i in VECTORS + (B_ONE,)}
    vectors = jnp.stack([low[i].reshape(8, width) for i in VECTORS], axis=1)
    vectors = jnp.pad(vectors, ((0, 0), (0, 0), (0, lanes - width)))
    vectors = jnp.concatenate([vectors, low[B_ONE].reshape(8, many, lanes)], axis=1)
    vectors = jnp.pad(vectors, ((0, 0), (0, rows - vectors.shape[1]), (0, 0)))
    shapes = [(rows, lanes)] + [params[i].shape for i in MATRICES]
    vectors = vectors.reshape(4, 2, HALVES, THIRDS, rows // 6, lanes)
    sums = reduce_all(vectors, [grads[i] for i in MATRICES])
    sums = [s.reshape(shape).astype(jnp.float32) for s, shape in zip(sums, shapes)]
    owned = [None] * len(params)
    for at, i in enumerate(VECTORS):
        owned[i] = sums[0][at, :width]
    owned[B_ONE] = sums[0][len(VECTORS) : len(VECTORS) + many].reshape(-1)
    for at, i in enumerate(MATRICES):
        owned[i] = sums[1 + at]
    return (result, grad_input) + tuple(owned)


def solution(mesh):
    in_specs = (
        P(("rep", "shard"), None),
        P(("rep", "shard")),
        P(("rep", "shard"), None),
        P("shard"),
        P("shard"),
        P("shard", None),
        P("shard", None),
        P("shard", None),
        P("shard"),
        P("shard"),
        P("shard", None),
        P("shard"),
        P("shard"),
        P("shard"),
        P("shard", None),
        P("shard"),
        P("shard", None),
        P("shard"),
    )
    out_specs = (
        P(("rep", "shard"), None),
        P(("rep", "shard"), None),
        P("shard"),
        P("shard"),
        P("shard", None),
        P("shard", None),
        P("shard", None),
        P("shard"),
        P("shard"),
        P("shard", None),
        P("shard"),
        P("shard"),
        P("shard"),
        P("shard", None),
        P("shard"),
        P("shard", None),
        P("shard"),
    )
    shape = dict(mesh.shape)
    fits = shape["rep"] == 4 and shape["shard"] == 8
    return jax.shard_map(
        on_device if fits else on_device_plain, mesh=mesh, in_specs=in_specs, out_specs=out_specs, check_vma=False
    )
```
